512 devices in a mesh: inst: 16 (over z, core), sp: 32 (over x, y).
Axes of the slice: x: 4, y: 8, z: 8, core: 2. Of those that a mesh axis runs over, the one named last changes fastest.
Arguments:
- prompt_queries: bfloat16 [16, 768, 4096], P('inst', None, 'sp')
- prompt_keys: bfloat16 [16, 768, 512], P('inst', 'sp')
- prompt_values: bfloat16 [16, 768, 512], P('inst', 'sp'), may hold values from -6 to 6
- span_of: int32 [16], replicated, may hold values from 0 to 15, each once
- short_queries: bfloat16 [16, 512, 4096], P('inst', None, 'sp')
- short_keys: bfloat16 [16, 512, 512], P('inst', 'sp')
- short_values: bfloat16 [16, 512, 512], P('inst', 'sp'), may hold values from -6 to 6
- short_lengths: int32 [16, 8], replicated, may hold values from 1 to 128, 512 in all within a row
- pair_partner: int32 [16], replicated, may hold values from 0 to 15, as said below
Outputs:
- prompt_out: bfloat16 [16, 768, 4096], P('inst', None, 'sp')
- short_out: bfloat16 [16, 512, 4096], P('inst', None, 'sp')
The draws below stay inside these ranges and needn't reach their ends.
Inputs may be any that keep to these rules, and one draw needn't show every extreme that they name: pair_partner is a permutation of the groups. `short_lengths`: each group's lengths sum to 512.
All inputs are finite; a program needn't handle non-finite values.
Results may differ from the reference program's by a relative error of at most 0.006.
Values may be sent and summed in bfloat16 or wider, within the bound.
No kernel may reach another device: no remote copies, remote signals or barrier semaphores. Data moves between devices by JAX's collectives and lax.ppermute only.
A program may use at most 64 MiB of HBM per device.

```python
import math
import jax
import jax.numpy as jnp
import numpy as np
from jax import lax

DH = 128
QH = 32
KVH = 4
SPAN = 768
SHORT = 512
NSEG = 8
N_INST = 16


def key_field(key, offset, rows):
    return jax.random.normal(jax.random.fold_in(key, offset), (N_INST, rows, KVH * DH), jnp.float32)


def place_aligned(plain, key, rows):
    chosen = (jnp.arange(rows) % 61 == 7)[None, :, None]
    return jnp.where(chosen, plain, plain)


def draw_prompt_keys(key, part):
    return key_field(key, 101, SPAN).astype(jnp.bfloat16)


def draw_short_keys(key, part):
    return key_field(key, 202, SHORT).astype(jnp.bfloat16)


def draw_prompt_queries(key, part):
    key = jax.random.fold_in(key, 3)
    shape = (N_INST, SPAN, QH * DH)
    plain = jax.random.normal(key, shape, jnp.float32)
    return place_aligned(plain, jax.random.fold_in(key, 7), SPAN).astype(jnp.bfloat16)


def draw_short_queries(key, part):
    key = jax.random.fold_in(key, 4)
    shape = (N_INST, SHORT, QH * DH)
    plain = jax.random.normal(key, shape, jnp.float32)
    return place_aligned(plain, jax.random.fold_in(key, 8), SHORT).astype(jnp.bfloat16)


def draw_pair_partner(key, part):
    key = jax.random.fold_in(key, 9)
    shuffled = jax.random.permutation(jax.random.fold_in(key, 1), N_INST).astype(jnp.int32)
    anchor = jax.random.randint(jax.random.fold_in(key, 2), (), 0, N_INST, dtype=jnp.int32)
    target = (anchor + N_INST // 2) % N_INST
    displaced = shuffled[anchor]
    places = jnp.arange(N_INST, dtype=jnp.int32)
    return jnp.where(places == anchor, target, jnp.where(shuffled == target, displaced, shuffled)).astype(jnp.int32)


def shard_levels(rng, dims, cuts, smallest, top_value):
    gain, own = 1.0, jax.random.fold_in(rng, 6)
    for position, blocks in cuts:
        heights = jnp.exp(jax.random.uniform(jax.random.fold_in(own, position), (blocks,), jnp.float32, smallest / len(cuts), top_value / len(cuts)))
        gain = gain * jnp.repeat(heights, dims[position] // blocks).reshape([-1 if axis == position else 1 for axis in range(len(dims))])
    return gain


def split_up(amount, total, reach, skew):
    loads = [(1 << 20) // math.isqrt(grade ** skew) + 1 for grade in range(2, amount + 1)]
    surplus, counts = total - reach - (amount - 1), [1] * (amount - 1)
    while surplus > 0:
        movable = [i for i in range(amount - 1) if counts[i] < reach]
        pool, remaining = sum([loads[i] for i in movable]), surplus
        for i in movable:
            more = min(reach - counts[i], max(1, remaining * loads[i] // pool), surplus)
            counts[i] = counts[i] + more
            surplus = surplus - more
    return np.array([reach] + counts)


def ragged(rng, number_of, total, reach, skew):
    if number_of == 2:
        one = jax.random.randint(rng, (), max(1, total - reach), min(reach, total - 1) + 1)
        return jnp.stack([one, total - one])
    lengths = jnp.asarray(split_up(number_of, total, reach, skew), jnp.int32)
    pairs = (number_of - 1) // 2
    giver, taker = lengths[1:1 + 2 * pairs:2], lengths[2:2 + 2 * pairs:2]
    slack = jnp.minimum(giver - 1, reach - taker)
    passed = jax.random.randint(jax.random.fold_in(rng, 1), (pairs,), 0, 1 << 20) % (slack + 1)
    lengths = lengths.at[1:1 + 2 * pairs:2].set(giver - passed).at[2:2 + 2 * pairs:2].set(taker + passed)
    return lengths[jax.random.permutation(jax.random.fold_in(rng, 2), number_of)]


def bell_draw(stream_key, shape, scale, limit, pieces=(), held_as=jnp.bfloat16):
    array = scale * jax.random.normal(stream_key, shape, jnp.float32)
    if pieces:
        array = array * shard_levels(stream_key, shape, pieces, -0.22, 0.18)
    return jnp.clip(array, -limit, limit).astype(held_as)


def setup_inputs(seed: int = 0) -> dict:
    key_of = jax.random.split(jax.random.key(seed), 10)
    return {
        "prompt_queries": draw_prompt_queries(jax.random.fold_in(key_of[9], 71), 0),
        "prompt_keys": draw_prompt_keys(jax.random.fold_in(key_of[9], 71), 0),
        "prompt_values": bell_draw(key_of[2], (N_INST, SPAN, KVH * DH), 1.0, 6.0, ((0, 16), (1, 32))),
        "span_of": jax.random.permutation(key_of[3], N_INST).astype(jnp.int32),
        "short_queries": draw_short_queries(jax.random.fold_in(key_of[9], 71), 0),
        "short_keys": draw_short_keys(jax.random.fold_in(key_of[9], 71), 0),
        "short_values": bell_draw(key_of[6], (N_INST, SHORT, KVH * DH), 1.0, 6.0, ((0, 16), (1, 32))),
        "short_lengths": jax.vmap(lambda own: ragged(own, NSEG, SHORT, SHORT // 4, 2))(jax.random.split(key_of[7], N_INST)).reshape((N_INST, NSEG)).astype(jnp.int32),
        "pair_partner": draw_pair_partner(jax.random.fold_in(key_of[9], 71), 0),
    }


def heads_first(matrix, count):
    return matrix.reshape(matrix.shape[0], count, DH).transpose(1, 0, 2)


def attend(query_heads, keys_t, values_t, visible):
    group = QH // KVH

    def per_head(inputs):
        query_head, head_index = inputs
        key_head = lax.dynamic_index_in_dim(keys_t, head_index // group, 0, keepdims=False)
        value_head = lax.dynamic_index_in_dim(values_t, head_index // group, 0, keepdims=False)
        scores = jnp.dot(query_head, key_head.T, preferred_element_type=jnp.float32) * DH ** -0.5
        scores = jnp.where(visible, scores, -jnp.inf)
        row_max = jnp.max(scores, axis=1, keepdims=True)
        weights = jnp.exp(scores - row_max)
        summed = jnp.dot(weights.astype(jnp.bfloat16), value_head, preferred_element_type=jnp.float32)
        return summed / jnp.sum(weights, axis=1, keepdims=True)

    return lax.map(per_head, (query_heads, jnp.arange(QH, dtype=jnp.int32)))


def reference(prompt_queries, prompt_keys, prompt_values, span_of, short_queries, short_keys, short_values, short_lengths, pair_partner):
    keys_t = heads_first(prompt_keys.reshape(N_INST * SPAN, KVH * DH), KVH)
    values_t = heads_first(prompt_values.reshape(N_INST * SPAN, KVH * DH), KVH)
    row_ids = jnp.arange(SPAN, dtype=jnp.int32)
    key_pos = (span_of[:, None] * SPAN + row_ids[None, :]).reshape(-1)

    def prompt_group(group_index):
        query_pos = span_of[group_index] * SPAN + row_ids
        visible = key_pos[None, :] <= query_pos[:, None]
        result = attend(heads_first(prompt_queries[group_index], QH), keys_t, values_t, visible)
        return result.transpose(1, 0, 2).reshape(SPAN, QH * DH).astype(jnp.bfloat16)

    prompt_out = lax.map(prompt_group, jnp.arange(N_INST, dtype=jnp.int32))
    short_ids = jnp.arange(SHORT, dtype=jnp.int32)

    def short_group(group_index):
        source = pair_partner[group_index]
        seg_ends = jnp.cumsum(short_lengths[source])
        seg_ids = jnp.sum((short_ids[:, None] >= seg_ends[None, :]).astype(jnp.int32), axis=1)
        visible = (seg_ids[:, None] == seg_ids[None, :]) & (short_ids[None, :] <= short_ids[:, None])
        result = attend(heads_first(short_queries[source], QH), heads_first(short_keys[source], KVH), heads_first(short_values[source], KVH), visible)
        return result.transpose(1, 0, 2).reshape(SHORT, QH * DH).astype(jnp.bfloat16)

    short_out = lax.map(short_group, jnp.arange(N_INST, dtype=jnp.int32))
    return prompt_out, short_out
```

```python
import functools

import jax
import jax.numpy as jnp
from jax import lax
from jax.experimental import pallas as pl
from jax.experimental.pallas import tpu as pltpu
from jax.sharding import PartitionSpec as P

DH = 128
QH = 32
KVH = 4
TILE = 256
LOG2E = 1.4426950408889634
GAIN = DH ** (-0.5) * LOG2E
VMEM = 48 * 1024 * 1024


def with_ones(values):
    return jnp.concatenate([values, jnp.ones_like(values)], axis=1)


def scores_of(q, keys):
    return lax.dot_general(q, keys, (((1,), (1,)), ((), ())), preferred_element_type=jnp.float32)


def weigh(weights, values):
    return jnp.dot(
        weights.astype(jnp.bfloat16), with_ones(values), preferred_element_type=jnp.float32
    )


def diagonal_kernel(q_ref, kv_ref, acc_ref, max_ref):
    for start in range(0, q_ref.shape[0], TILE):
        rows = pl.ds(start, TILE)
        seen = start + TILE
        scores = scores_of(q_ref[rows, :], kv_ref[:seen, :DH])
        row = start + lax.broadcasted_iota(jnp.int32, scores.shape, 0)
        col = lax.broadcasted_iota(jnp.int32, scores.shape, 1)
        scores = jnp.where(col <= row, scores, -jnp.inf)
        top = jnp.max(scores, axis=1, keepdims=True)
        weights = jnp.exp2((scores - top) * GAIN)
        acc_ref[rows, :] = weigh(weights, kv_ref[:seen, DH:])
        max_ref[rows, :] = jnp.broadcast_to(top, (TILE, DH))


def short_kernel(lengths_ref, q_ref, kv_ref, out_ref):
    ends = []
    total = 0
    for k in range(lengths_ref.shape[0]):
        total = total + lengths_ref[k]
        ends.append(total)
    for start in range(0, q_ref.shape[0], TILE):
        rows = pl.ds(start, TILE)
        seen = start + TILE
        scores = scores_of(q_ref[rows, :], kv_ref[:seen, :DH])
        row = start + lax.broadcasted_iota(jnp.int32, (TILE, 1), 0)
        first = jnp.zeros((TILE, 1), jnp.int32)
        for end in ends:
            first = jnp.where(row >= end, end, first)
        col = lax.broadcasted_iota(jnp.int32, scores.shape, 1)
        scores = jnp.where((col <= row) & (col >= first), scores, -jnp.inf)
        top = jnp.max(scores, axis=1, keepdims=True)
        weights = jnp.exp2((scores - top) * GAIN)
        acc = weigh(weights, kv_ref[:seen, DH:])
        out_ref[rows, :] = (acc[:, :DH] / acc[:, DH:]).astype(jnp.bfloat16)


def earlier_kernel(order_ref, count_ref, q_ref, kv_ref, acc0_ref, max0_ref, out_ref, acc, top):
    step = pl.program_id(0)

    @pl.when(step == 0)
    def _():
        acc[...] = acc0_ref[...]
        top[...] = max0_ref[:, :1]

    @pl.when(step < count_ref[0])
    def _():
        for start in range(0, q_ref.shape[0], TILE):
            rows = pl.ds(start, TILE)
            scores = scores_of(q_ref[rows, :], kv_ref[0, :, :DH])
            old = top[rows, :]
            new = jnp.maximum(old, jnp.max(scores, axis=1, keepdims=True))
            weights = jnp.exp2((scores - new) * GAIN)
            factor = jnp.exp2((old - new) * GAIN)
            acc[rows, :] = acc[rows, :] * factor + weigh(weights, kv_ref[0, :, DH:])
            top[rows, :] = new

    @pl.when(step == pl.num_programs(0) - 1)
    def _():
        out_ref[...] = (acc[:, :DH] / acc[:, DH:]).astype(jnp.bfloat16)


def diagonal(q, kv):
    rows = q.shape[0]
    return pl.pallas_call(
        diagonal_kernel,
        out_shape=(
            jax.ShapeDtypeStruct((rows, 2 * DH), jnp.float32),
            jax.ShapeDtypeStruct((rows, DH), jnp.float32),
        ),
        compiler_params=pltpu.CompilerParams(vmem_limit_bytes=VMEM),
        cost_estimate=pl.CostEstimate(flops=2 * rows * rows * DH, bytes_accessed=4 * rows * 1024, transcendentals=rows * rows // 2),
        name="diagonal",
    )(q, kv)


def shorts(lengths, q, kv):
    rows = q.shape[0]
    return pl.pallas_call(
        short_kernel,
        out_shape=jax.ShapeDtypeStruct((rows, DH), jnp.bfloat16),
        in_specs=[
            pl.BlockSpec(memory_space=pltpu.SMEM),
            pl.BlockSpec(memory_space=pltpu.VMEM),
            pl.BlockSpec(memory_space=pltpu.VMEM),
        ],
        compiler_params=pltpu.CompilerParams(vmem_limit_bytes=VMEM),
        cost_estimate=pl.CostEstimate(flops=2 * rows * rows * DH, bytes_accessed=rows * 1024, transcendentals=rows * rows // 2),
        name="shorts",
    )(lengths, q, kv)


def earlier(order, count, q, kv_all, acc, top):
    groups, rows, width = kv_all.shape
    whole = lambda j, order, count: (0, 0)
    return pl.pallas_call(
        earlier_kernel,
        out_shape=jax.ShapeDtypeStruct((rows, DH), jnp.bfloat16),
        grid_spec=pltpu.PrefetchScalarGridSpec(
            num_scalar_prefetch=2,
            grid=(groups,),
            in_specs=[
                pl.BlockSpec((rows, DH), whole),
                pl.BlockSpec((1, rows, width), lambda j, order, count: (order[j], 0, 0)),
                pl.BlockSpec((rows, 2 * DH), whole),
                pl.BlockSpec((rows, DH), whole),
            ],
            out_specs=pl.BlockSpec((rows, DH), whole),
            scratch_shapes=[
                pltpu.VMEM((rows, 2 * DH), jnp.float32),
                pltpu.VMEM((rows, 1), jnp.float32),
            ],
        ),
        compiler_params=pltpu.CompilerParams(vmem_limit_bytes=VMEM),
        cost_estimate=pl.CostEstimate(
            flops=2 * 8 * 2 * rows * rows * DH, bytes_accessed=groups * rows * width * 2, transcendentals=8 * rows * rows
        ),
        name="earlier",
    )(order, count, q, kv_all, acc, top)


def reorder_kernel(index_ref, blocks_ref, out_ref):
    for slot in range(out_ref.shape[0]):
        out_ref[slot] = blocks_ref[index_ref[slot]]


def reorder(index, blocks):
    return pl.pallas_call(
        reorder_kernel,
        out_shape=jax.ShapeDtypeStruct(blocks.shape, blocks.dtype),
        in_specs=[
            pl.BlockSpec(memory_space=pltpu.SMEM),
            pl.BlockSpec(memory_space=pltpu.VMEM),
        ],
        name="reorder",
    )(index, blocks)


def by_head(keys, values, copies):
    rows = keys.shape[0]
    both = jnp.concatenate(
        [keys.reshape(rows, KVH, DH), values.reshape(rows, KVH, DH)], axis=2
    ).transpose(1, 0, 2)
    return jnp.broadcast_to(both[:, None], (KVH, copies, rows, 2 * DH)).reshape(
        KVH * copies, rows, 2 * DH
    )


def swapped(blocks, axis):
    return lax.all_to_all(blocks, axis, split_axis=0, concat_axis=0, tiled=True)


def body(
    prompt_queries,
    prompt_keys,
    prompt_values,
    span_of,
    short_queries,
    short_keys,
    short_values,
    short_lengths,
    pair_partner,
):
    groups = lax.axis_size("inst")
    me = lax.axis_index("inst")
    copies = lax.axis_size("sp") // KVH
    span_rows = prompt_queries.shape[1]
    short_rows = short_queries.shape[1]

    own = swapped(by_head(prompt_keys[0], prompt_values[0], copies), "sp")
    own = own.reshape(span_rows, 2 * DH)
    everyone = lax.all_gather(own, "inst", axis=0, tiled=False)

    short_keys, short_values, own = lax.optimization_barrier((short_keys, short_values, own))
    acc, top = diagonal(prompt_queries[0], own)

    short_own = swapped(by_head(short_keys[0], short_values[0], copies), "sp")
    short_own = short_own.reshape(short_rows, 2 * DH)
    served = shorts(short_lengths[me], short_queries[0], short_own)
    pieces = swapped(served.reshape(groups, short_rows // groups, DH), "inst")
    pieces = swapped(reorder(pair_partner, pieces), "inst")
    short_out = pieces.reshape(1, short_rows, DH)

    my_span = span_of[me]
    ids = jnp.arange(groups, dtype=jnp.int32)
    holder = jnp.sum(jnp.where(span_of[None, :] == ids[:, None], ids[None, :], 0), axis=1)
    last = jnp.maximum(my_span - 1, 0)
    order = jnp.where(ids <= last, holder, jnp.sum(jnp.where(ids == last, holder, 0)))
    prompt_out = earlier(order, my_span[None], prompt_queries[0], everyone, acc, top)
    return (prompt_out[None], short_out)


def solution(mesh):
    placed = (
        P("inst", None, "sp"),
        P("inst", "sp", None),
        P("inst", "sp", None),
        P(),
        P("inst", None, "sp"),
        P("inst", "sp", None),
        P("inst", "sp", None),
        P(),
        P(),
    )
    return jax.shard_map(
        body,
        mesh=mesh,
        in_specs=placed,
        out_specs=(P("inst", None, "sp"), P("inst", None, "sp")),
        check_vma=False,
    )
```

```python
import functools

import jax
import jax.numpy as jnp
from jax import lax
from jax.experimental import pallas as pl
from jax.experimental.pallas import tpu as pltpu
from jax.sharding import PartitionSpec as P

DH = 128
QH = 32
KVH = 4
CORES = 2
TILE = 128
SHORT_TILE = 256
LOG2E = 1.4426950408889634
GAIN = DH ** (-0.5) * LOG2E
VMEM = 48 * 1024 * 1024
SMEM_SPEC = pl.BlockSpec(memory_space=pltpu.SMEM)
VMEM_SPEC = pl.BlockSpec(memory_space=pltpu.VMEM)


def with_ones(values):
    return jnp.concatenate([values, jnp.ones_like(values)], axis=1)


def scores_of(q, keys):
    return lax.dot_general(q, keys, (((1,), (1,)), ((), ())), preferred_element_type=jnp.float32)


def weigh(weights, values):
    return jnp.dot(
        weights.astype(jnp.bfloat16), with_ones(values), preferred_element_type=jnp.float32
    )


def add_block(q_ref, keys_t, values, state):
    tiles = [pl.ds(start, TILE) for start in range(0, q_ref.shape[0], TILE)]
    values = with_ones(values)
    scores = [jnp.dot(q_ref[rows, :], keys_t, preferred_element_type=jnp.float32) for rows in tiles]
    olds = [state[rows, 2 * DH : 2 * DH + 1] for rows in tiles]
    parts = []
    for score, old in zip(scores, olds):
        new = jnp.maximum(old, jnp.max(score, axis=1, keepdims=True))
        weights = jnp.exp2((score - new) * GAIN).astype(jnp.bfloat16)
        parts.append((new, jnp.exp2((old - new) * GAIN), weights))
    for rows, (new, factor, weights) in zip(tiles, parts):
        added = jnp.dot(weights, values, preferred_element_type=jnp.float32)
        state[rows, : 2 * DH] = state[rows, : 2 * DH] * factor + added
        state[rows, 2 * DH :] = jnp.broadcast_to(new, (TILE, DH))


def diagonal(q_ref, keys_t, kv_ref, state):
    for start in range(0, q_ref.shape[0], TILE):
        rows = pl.ds(start, TILE)
        seen = start + TILE
        scores = jnp.dot(q_ref[rows, :], keys_t[:, :seen], preferred_element_type=jnp.float32)
        row = start + lax.broadcasted_iota(jnp.int32, scores.shape, 0)
        col = lax.broadcasted_iota(jnp.int32, scores.shape, 1)
        scores = jnp.where(col <= row, scores, -jnp.inf)
        top = jnp.max(scores, axis=1, keepdims=True)
        weights = jnp.exp2((scores - top) * GAIN)
        state[rows, : 2 * DH] = weigh(weights, kv_ref[:seen, DH:])
        state[rows, 2 * DH :] = jnp.broadcast_to(top, (TILE, DH))


def own_kernel(seen_ref, q_ref, other_q_ref, kv_ref, state, other, keys_t):
    keys_t[...] = kv_ref[: q_ref.shape[0], :DH].T
    diagonal(q_ref, keys_t, kv_ref, state)
    other[:, : 2 * DH] = jnp.zeros((other.shape[0], 2 * DH), jnp.float32)
    other[:, 2 * DH :] = jnp.full((other.shape[0], DH), -jnp.inf, jnp.float32)

    @pl.when(seen_ref[1, 0] > 0)
    def _():
        add_block(other_q_ref, keys_t[...], kv_ref[: q_ref.shape[0], DH:], other)


def ring_kernel(seen_ref, q_ref, other_q_ref, *refs, indices):
    kv_refs, (before, other_before, state, other, keys_t) = refs[:-5], refs[-5:]
    state[...] = before[...]
    other[...] = other_before[...]
    for index, kv_ref in zip(indices, kv_refs):

        @pl.when((seen_ref[0, index] > 0) | (seen_ref[1, index] > 0))
        def _():
            keys_t[...] = kv_ref[: q_ref.shape[0], :DH].T

        @pl.when(seen_ref[0, index] > 0)
        def _():
            add_block(q_ref, keys_t[...], kv_ref[: q_ref.shape[0], DH:], state)

        @pl.when(seen_ref[1, index] > 0)
        def _():
            add_block(other_q_ref, keys_t[...], kv_ref[: q_ref.shape[0], DH:], other)


def fetch(slot, riders, target, sem):
    for k, ref in enumerate(riders):

        @pl.when(slot == k)
        def _():
            load = pltpu.make_async_copy(ref.at[pl.ds(ref.shape[0] - target.shape[0], target.shape[0]), :], target, sem)
            load.start()
            load.wait()


def end_kernel(seen_ref, slot_ref, q_ref, kv_ref, before, *refs, which, index):
    riders, (packed, state, keys_t, rider, sem) = refs[:-5], refs[-5:]
    rows = q_ref.shape[0]
    state[...] = before[...]

    @pl.when(seen_ref[which, index] > 0)
    def _():
        keys_t[...] = kv_ref[:rows, :DH].T
        add_block(q_ref, keys_t[...], kv_ref[:rows, DH:], state)

    packed[:rows, :DH] = state[:, :DH]
    lane = lax.broadcasted_iota(jnp.int32, (rows, DH), 1)
    packed[:rows, DH:] = jnp.where(lane < DH // 2, state[:, DH : 2 * DH], state[:, 2 * DH :])
    if riders:
        rider[...] = jnp.zeros(rider.shape, rider.dtype)
        fetch(slot_ref[which], riders, rider, sem)
        packed[rows:, :] = rider[...].astype(jnp.float32)


def merge_kernel(slot_ref, mine_ref, other_ref, *refs):
    riders, (out, short_out, rider, sem) = refs[:-4], refs[-4:]
    total = out.shape[0]
    rider[...] = other_ref[total:, :].astype(jnp.bfloat16)
    fetch(slot_ref[0], riders, rider, sem)
    half = rider.shape[0]
    short_out[:half, :] = rider[:, :DH]
    short_out[half:, :] = rider[:, DH:]
    for start in range(0, total, TILE):
        rows = pl.ds(start, TILE)
        mine = mine_ref[rows, 2 * DH - 1 :]
        other = other_ref[rows, 2 * DH - 1 :]
        top = jnp.maximum(mine, other)
        mine = jnp.exp2((mine - top) * GAIN)
        other = jnp.exp2((other - top) * GAIN)
        sums = mine_ref[rows, :DH] * mine + other_ref[rows, :DH] * other
        weight = mine_ref[rows, DH : DH + 1] * mine + other_ref[rows, DH : DH + 1] * other
        out[rows, :] = (sums / weight).astype(jnp.bfloat16)


def load_kernel(lengths_ref, q_ref, kv_ref, own_ref, out_ref):
    out_ref[: own_ref.shape[0], :] = own_ref[...]
    half = q_ref.shape[0] // 2
    ends = []
    total = 0
    for k in range(lengths_ref.shape[0]):
        total = total + lengths_ref[k]
        ends.append(total)
    for start in range(0, q_ref.shape[0], SHORT_TILE):
        rows = pl.ds(start, SHORT_TILE)
        seen = start + SHORT_TILE
        scores = scores_of(q_ref[rows, :], kv_ref[:seen, :DH])
        row = start + lax.broadcasted_iota(jnp.int32, (SHORT_TILE, 1), 0)
        first = jnp.zeros((SHORT_TILE, 1), jnp.int32)
        for end in ends:
            first = jnp.where(row >= end, end, first)
        col = lax.broadcasted_iota(jnp.int32, scores.shape, 1)
        scores = jnp.where((col <= row) & (col >= first), scores, -jnp.inf)
        top = jnp.max(scores, axis=1, keepdims=True)
        weights = jnp.exp2((scores - top) * GAIN)
        acc = weigh(weights, kv_ref[:seen, DH:])
        columns = slice(0, DH) if start < half else slice(DH, 2 * DH)
        place = pl.ds(own_ref.shape[0] + start % half, SHORT_TILE)
        out_ref[place, columns] = (acc[:, :DH] / acc[:, DH:]).astype(jnp.bfloat16)


def call(kernel, out_shape, operands, name, scratch=(), left=0):
    specs = [SMEM_SPEC if x.dtype == jnp.int32 else VMEM_SPEC for x in operands]
    return pl.pallas_call(
        kernel,
        out_shape=out_shape,
        in_specs=specs[: len(specs) - left] + [pl.BlockSpec(memory_space=pl.ANY)] * left,
        out_specs=jax.tree.map(lambda _: VMEM_SPEC, out_shape),
        scratch_shapes=scratch,
        compiler_params=pltpu.CompilerParams(vmem_limit_bytes=VMEM),
        cost_estimate=pl.CostEstimate(flops=1, bytes_accessed=1, transcendentals=0),
        name=name,
    )(*operands)


def state_of(rows, width=3 * DH):
    return jax.ShapeDtypeStruct((rows, width), jnp.float32)


def heads_kernel(short_keys, short_values, keys, values, out):
    cut = short_keys.shape[0]
    copies = out.shape[0] // KVH
    for head in range(KVH):
        columns = slice(head * DH, (head + 1) * DH)
        block = jnp.concatenate(
            [
                jnp.concatenate([short_keys[:, columns], short_values[:, columns]], axis=1),
                jnp.concatenate([keys[:, columns], values[:, columns]], axis=1),
            ],
            axis=0,
        )
        for copy in range(copies):
            out[head * copies + copy] = block


def swapped(blocks, axis):
    return lax.all_to_all(blocks, axis, split_axis=0, concat_axis=0, tiled=True)


def across(block):
    return lax.ppermute(block, "inst", [(i, i ^ 1) for i in range(lax.axis_size("inst"))])


def ahead(block):
    size = lax.axis_size("inst")
    step = lambda i: CORES if i % CORES == 0 else -CORES
    return lax.ppermute(block, "inst", [(i, (i + step(i)) % size) for i in range(size)])


def body(
    prompt_queries,
    prompt_keys,
    prompt_values,
    span_of,
    short_queries,
    short_keys,
    short_values,
    short_lengths,
    pair_partner,
):
    groups = lax.axis_size("inst")
    chips = groups // CORES
    me = lax.axis_index("inst")
    rows = prompt_queries.shape[1]
    short_rows = short_queries.shape[1]
    queries = prompt_queries[0]

    cut = short_keys.shape[1]
    heads = pl.pallas_call(
        heads_kernel,
        out_shape=jax.ShapeDtypeStruct(
            (lax.axis_size("sp"), cut + prompt_keys.shape[1], 2 * DH), jnp.bfloat16
        ),
        name="heads",
    )(short_keys[0], short_values[0], prompt_keys[0], prompt_values[0])
    got = swapped(heads, "sp")
    short_own = got[:, :cut].reshape(short_rows, 2 * DH)
    own = got[:, cut:].reshape(rows, 2 * DH)
    own, short_own, other_queries = lax.optimization_barrier((own, short_own, across(queries)))
    load = call(
        load_kernel,
        jax.ShapeDtypeStruct((rows + short_rows // 2, 2 * DH), jnp.bfloat16),
        (short_lengths[me], short_queries[0], short_own, own),
        "load",
    )
    ring = [(load, across(load))]
    for step in range(1, chips // 2):
        ring.append(tuple(ahead(block) for block in ring[-1]))
    end = ahead(ring[-1][0])
    core = me % CORES
    chip = me // CORES + jnp.asarray(range(chips // 2 + 1), jnp.int32) * (2 * core - 1)
    held = (chip % chips * CORES)[:, None] + jnp.stack([core, 1 - core])[None, :]
    held = held.reshape(-1)
    ids = jnp.arange(groups, dtype=jnp.int32)
    spans = jnp.sum(jnp.where(held[:, None] == ids[None, :], span_of[None, :], 0), axis=1)
    mine = jnp.stack([span_of[me], span_of[me ^ 1]])
    seen = (spans[None, :] < mine[:, None]).astype(jnp.int32)

    riders = [block for pair in ring for block in pair] + [end]
    wanted = jnp.stack([pair_partner[me], pair_partner[me ^ 1]])
    found = held[None, : len(riders)] == wanted[:, None]
    slots = jnp.arange(len(riders), dtype=jnp.int32)
    slot = jnp.min(jnp.where(found, slots[None, :], len(riders)), axis=1)

    keys_t = pltpu.VMEM((DH, rows), jnp.bfloat16)
    both = (state_of(rows), state_of(rows))

    def ring_step(step, state, other):
        return call(
            functools.partial(ring_kernel, indices=(2 * step, 2 * step + 1)),
            both,
            (seen, queries, other_queries, *ring[step], state, other),
            "ring",
            [keys_t],
        )

    state, other = call(own_kernel, both, (seen, queries, other_queries, load), "own", [keys_t])
    for step in range(1, chips // 2):
        state, other = ring_step(step, state, other)

    rider_space = [pltpu.VMEM((short_rows // 2, 2 * DH), jnp.bfloat16), pltpu.SemaphoreType.DMA]
    end_space = [pltpu.VMEM((rows, 3 * DH), jnp.float32), keys_t] + rider_space

    def ending(which, q, before, riders):
        return call(
            functools.partial(end_kernel, which=which, index=chips),
            state_of(rows + (short_rows // 2 if riders else 0), 2 * DH),
            (seen, slot, q, end, before, *riders),
            "end",
            end_space,
            len(riders),
        )

    other = across(ending(1, other_queries, other, riders))
    state = ending(0, queries, state, [])
    prompt_out, short_out = call(
        merge_kernel,
        (jax.ShapeDtypeStruct((rows, DH), jnp.bfloat16), jax.ShapeDtypeStruct((short_rows, DH), jnp.bfloat16)),
        (slot, state, other, *riders),
        "merge",
        rider_space,
        len(riders),
    )
    return (prompt_out[None], short_out[None])


def solution(mesh):
    placed = (
        P("inst", None, "sp"),
        P("inst", "sp", None),
        P("inst", "sp", None),
        P(),
        P("inst", None, "sp"),
        P("inst", "sp", None),
        P("inst", "sp", None),
        P(),
        P(),
    )
    return jax.shard_map(
        body,
        mesh=mesh,
        in_specs=placed,
        out_specs=(P("inst", None, "sp"), P("inst", None, "sp")),
        check_vma=False,
    )
```

```python
import functools

import jax
import jax.numpy as jnp
from jax import lax
from jax.experimental import pallas as pl
from jax.experimental.pallas import tpu as pltpu
from jax.sharding import PartitionSpec as P

DH = 128
QH = 32
KVH = 4
CORES = 2
TILE = 128
SHORT_TILE = 256
LOG2E = 1.4426950408889634
GAIN = DH ** (-0.5) * LOG2E
VMEM = 24 * 1024 * 1024
COST = {"load": 10**9, "own": 2 * 10**9, "ring": 4 * 10**9, "end": 10**9, "merge": 10**9}
SMEM_SPEC = pl.BlockSpec(memory_space=pltpu.SMEM)
VMEM_SPEC = pl.BlockSpec(memory_space=pltpu.VMEM)


def with_ones(values):
    return jnp.concatenate([values, jnp.ones_like(values)], axis=1)


def scores_of(q, keys):
    return lax.dot_general(q, keys, (((1,), (1,)), ((), ())), preferred_element_type=jnp.float32)


def weigh(weights, values):
    return jnp.dot(
        weights.astype(jnp.bfloat16), with_ones(values), preferred_element_type=jnp.float32
    )


def add_block(q_ref, keys_t, values, state):
    tiles = [pl.ds(start, TILE) for start in range(0, q_ref.shape[0], TILE)]
    values = with_ones(values)
    scores = [jnp.dot(q_ref[rows, :], keys_t, preferred_element_type=jnp.float32) for rows in tiles]
    olds = [state[rows, 2 * DH : 2 * DH + 1] for rows in tiles]
    parts = []
    for score, old in zip(scores, olds):
        new = jnp.maximum(old, jnp.max(score, axis=1, keepdims=True))
        weights = jnp.exp2((score - new) * GAIN).astype(jnp.bfloat16)
        parts.append((new, jnp.exp2((old - new) * GAIN), weights))
    for rows, (new, factor, weights) in zip(tiles, parts):
        added = jnp.dot(weights, values, preferred_element_type=jnp.float32)
        state[rows, : 2 * DH] = state[rows, : 2 * DH] * factor + added
        state[rows, 2 * DH :] = jnp.broadcast_to(new, (TILE, DH))


def diagonal(q_ref, keys_t, kv_ref, state):
    for start in range(0, q_ref.shape[0], TILE):
        rows = pl.ds(start, TILE)
        seen = start + TILE
        scores = jnp.dot(q_ref[rows, :], keys_t[:, :seen], preferred_element_type=jnp.float32)
        row = start + lax.broadcasted_iota(jnp.int32, scores.shape, 0)
        col = lax.broadcasted_iota(jnp.int32, scores.shape, 1)
        scores = jnp.where(col <= row, scores, -jnp.inf)
        top = jnp.max(scores, axis=1, keepdims=True)
        weights = jnp.exp2((scores - top) * GAIN)
        state[rows, : 2 * DH] = weigh(weights, kv_ref[:seen, DH:])
        state[rows, 2 * DH :] = jnp.broadcast_to(top, (TILE, DH))


def own_kernel(seen_ref, q_ref, other_q_ref, kv_ref, state, other, keys_t):
    keys_t[...] = kv_ref[: q_ref.shape[0], :DH].T
    diagonal(q_ref, keys_t, kv_ref, state)
    other[:, : 2 * DH] = jnp.zeros((other.shape[0], 2 * DH), jnp.float32)
    other[:, 2 * DH :] = jnp.full((other.shape[0], DH), -jnp.inf, jnp.float32)

    @pl.when(seen_ref[1, 0] > 0)
    def _():
        add_block(other_q_ref, keys_t[...], kv_ref[: q_ref.shape[0], DH:], other)


def ring_kernel(seen_ref, q_ref, other_q_ref, *refs, indices):
    kv_refs, (before, other_before, state, other, keys_t) = refs[:-5], refs[-5:]
    state[...] = before[...]
    other[...] = other_before[...]
    for index, kv_ref in zip(indices, kv_refs):

        @pl.when((seen_ref[0, index] > 0) | (seen_ref[1, index] > 0))
        def _():
            keys_t[...] = kv_ref[: q_ref.shape[0], :DH].T

        @pl.when(seen_ref[0, index] > 0)
        def _():
            add_block(q_ref, keys_t[...], kv_ref[: q_ref.shape[0], DH:], state)

        @pl.when(seen_ref[1, index] > 0)
        def _():
            add_block(other_q_ref, keys_t[...], kv_ref[: q_ref.shape[0], DH:], other)


def fetch(slot, riders, target, sem):
    for k, ref in enumerate(riders):

        @pl.when(slot == k)
        def _():
            load = pltpu.make_async_copy(ref.at[pl.ds(ref.shape[0] - target.shape[0], target.shape[0]), :], target, sem)
            load.start()
            load.wait()


def end_kernel(seen_ref, slot_ref, q_ref, kv_ref, before, *refs, which, index):
    riders, (packed, state, keys_t, rider, sem) = refs[:-5], refs[-5:]
    rows = q_ref.shape[0]
    state[...] = before[...]

    @pl.when(seen_ref[which, index] > 0)
    def _():
        keys_t[...] = kv_ref[:rows, :DH].T
        add_block(q_ref, keys_t[...], kv_ref[:rows, DH:], state)

    packed[:rows, :DH] = state[:, :DH]
    lane = lax.broadcasted_iota(jnp.int32, (rows, DH), 1)
    packed[:rows, DH:] = jnp.where(lane < DH // 2, state[:, DH : 2 * DH], state[:, 2 * DH :])
    if riders:
        rider[...] = jnp.zeros(rider.shape, rider.dtype)
        fetch(slot_ref[which], riders, rider, sem)
        packed[rows:, :] = rider[...].astype(jnp.float32)


def merge_kernel(slot_ref, mine_ref, other_ref, *refs):
    riders, (out, short_out, rider, sem) = refs[:-4], refs[-4:]
    total = out.shape[0]
    rider[...] = other_ref[total:, :].astype(jnp.bfloat16)
    fetch(slot_ref[0], riders, rider, sem)
    half = rider.shape[0]
    short_out[:half, :] = rider[:, :DH]
    short_out[half:, :] = rider[:, DH:]
    for start in range(0, total, TILE):
        rows = pl.ds(start, TILE)
        mine = mine_ref[rows, 2 * DH - 1 :]
        other = other_ref[rows, 2 * DH - 1 :]
        top = jnp.maximum(mine, other)
        mine = jnp.exp2((mine - top) * GAIN)
        other = jnp.exp2((other - top) * GAIN)
        sums = mine_ref[rows, :DH] * mine + other_ref[rows, :DH] * other
        weight = mine_ref[rows, DH : DH + 1] * mine + other_ref[rows, DH : DH + 1] * other
        out[rows, :] = (sums / weight).astype(jnp.bfloat16)


def load_kernel(ends_ref, q_ref, kv_ref, own_ref, out_ref):
    out_ref[: own_ref.shape[0], :] = own_ref[...]
    half = q_ref.shape[0] // 2
    for start in range(0, q_ref.shape[0], SHORT_TILE):
        rows = pl.ds(start, SHORT_TILE)
        seen = start + SHORT_TILE
        scores = scores_of(q_ref[rows, :], kv_ref[:seen, :DH])
        row = start + lax.broadcasted_iota(jnp.int32, (SHORT_TILE, 1), 0)
        first = jnp.zeros((SHORT_TILE, 1), jnp.int32)
        for k in range(ends_ref.shape[0]):
            first = jnp.where(row >= ends_ref[k], ends_ref[k], first)
        col = lax.broadcasted_iota(jnp.int32, scores.shape, 1)
        scores = jnp.where((col <= row) & (col >= first), scores, -jnp.inf)
        top = jnp.max(scores, axis=1, keepdims=True)
        weights = jnp.exp2((scores - top) * GAIN)
        acc = weigh(weights, kv_ref[:seen, DH:])
        columns = slice(0, DH) if start < half else slice(DH, 2 * DH)
        place = pl.ds(own_ref.shape[0] + start % half, SHORT_TILE)
        out_ref[place, columns] = (acc[:, :DH] / acc[:, DH:]).astype(jnp.bfloat16)


def call(kernel, out_shape, operands, name, scratch=(), left=0):
    specs = [SMEM_SPEC if x.dtype == jnp.int32 else VMEM_SPEC for x in operands]
    return pl.pallas_call(
        kernel,
        out_shape=out_shape,
        in_specs=specs[: len(specs) - left] + [pl.BlockSpec(memory_space=pl.ANY)] * left,
        out_specs=jax.tree.map(lambda _: VMEM_SPEC, out_shape),
        scratch_shapes=scratch,
        compiler_params=pltpu.CompilerParams(vmem_limit_bytes=VMEM),
        cost_estimate=pl.CostEstimate(flops=COST[name], bytes_accessed=1, transcendentals=0),
        name=name,
    )(*operands)


def plan_kernel(me_ref, span_ref, partner_ref, lengths_ref, seen_ref, slot_ref, ends_ref):
    groups = span_ref.shape[0]
    chips = groups // CORES
    me = me_ref[0]
    core = lax.rem(me, CORES)
    for which in range(CORES):
        rows = me if which == 0 else me + 1 - 2 * core
        wanted = partner_ref[rows]
        slot = jnp.int32(chips)
        for k in range(chips + 1):
            chip = lax.rem(me // CORES + (k // 2) * (2 * core - 1) + chips, chips)
            held = chip * CORES + (core if k % 2 == 0 else 1 - core)
            seen_ref[which, k] = (span_ref[held] < span_ref[rows]).astype(jnp.int32)
            if k != 1:
                slot = jnp.where(held == wanted, max(k - 1, 0), slot)
        slot_ref[which] = slot
    total = jnp.int32(0)
    for k in range(lengths_ref.shape[1]):
        total = total + lengths_ref[me, k]
        ends_ref[k] = total


def state_of(rows, width=3 * DH):
    return jax.ShapeDtypeStruct((rows, width), jnp.float32)


def heads_kernel(short_keys, short_values, keys, values, out):
    cut = short_keys.shape[0]
    copies = out.shape[0] // KVH
    for head in range(KVH):
        columns = slice(head * DH, (head + 1) * DH)
        block = jnp.concatenate(
            [
                jnp.concatenate([short_keys[:, columns], short_values[:, columns]], axis=1),
                jnp.concatenate([keys[:, columns], values[:, columns]], axis=1),
            ],
            axis=0,
        )
        for copy in range(copies):
            out[head * copies + copy] = block


def swapped(blocks, axis):
    return lax.all_to_all(blocks, axis, split_axis=0, concat_axis=0, tiled=True)


def across(block):
    return lax.ppermute(block, "inst", [(i, i ^ 1) for i in range(lax.axis_size("inst"))])


def ahead(block, crossing=False):
    size = lax.axis_size("inst")
    step = lambda i: CORES if (i + crossing) % CORES == 0 else -CORES
    return lax.ppermute(block, "inst", [(i, ((i ^ 1 if crossing else i) + step(i)) % size) for i in range(size)])


def body(
    prompt_queries,
    prompt_keys,
    prompt_values,
    span_of,
    short_queries,
    short_keys,
    short_values,
    short_lengths,
    pair_partner,
):
    groups = lax.axis_size("inst")
    chips = groups // CORES
    me = lax.axis_index("inst")
    rows = prompt_queries.shape[1]
    short_rows = short_queries.shape[1]
    queries = prompt_queries[0]

    cut = short_keys.shape[1]
    heads = pl.pallas_call(
        heads_kernel,
        out_shape=jax.ShapeDtypeStruct(
            (lax.axis_size("sp"), cut + prompt_keys.shape[1], 2 * DH), jnp.bfloat16
        ),
        name="heads",
    )(short_keys[0], short_values[0], prompt_keys[0], prompt_values[0])
    got = swapped(heads, "sp")
    short_own = got[:, :cut].reshape(short_rows, 2 * DH)
    own = got[:, cut:].reshape(rows, 2 * DH)
    ints = lambda *shape: jax.ShapeDtypeStruct(shape, jnp.int32)
    seen, slot, ends = pl.pallas_call(
        plan_kernel,
        out_shape=(ints(CORES, chips + 1), ints(CORES), ints(short_lengths.shape[1])),
        in_specs=[SMEM_SPEC] * 4,
        out_specs=(SMEM_SPEC,) * 3,
        name="plan",
    )(me[None], span_of, pair_partner, short_lengths)
    own, short_own, other_queries = lax.optimization_barrier((own, short_own, across(queries)))
    load = call(
        load_kernel,
        jax.ShapeDtypeStruct((rows + short_rows // 2, 2 * DH), jnp.bfloat16),
        (ends, short_queries[0], short_own, own),
        "load",
    )
    keys_t = pltpu.VMEM((DH, rows), jnp.bfloat16)
    both = (state_of(rows), state_of(rows))

    def ring_step(step, states):
        return call(
            functools.partial(ring_kernel, indices=(2 * step, 2 * step + 1)),
            both,
            (seen, queries, other_queries, *ring[step], *states),
            "ring",
            [keys_t],
        )

    states = call(own_kernel, both, (seen, queries, other_queries, load), "own", [keys_t])
    ring = [(load,), (ahead(load), ahead(load, crossing=True))]
    ring.append(tuple(ahead(block) for block in ring[1]))
    even, states = lax.optimization_barrier((ring[2][0], states))
    ring.append((ahead(even), ahead(ring[2][1])))
    end = ahead(ring[3][0])
    for step in range(1, chips // 2):
        states = ring_step(step, states)
    state, other = states

    riders = [block for pair in ring for block in pair] + [end]
    rider_space = [pltpu.VMEM((short_rows // 2, 2 * DH), jnp.bfloat16), pltpu.SemaphoreType.DMA]
    end_space = [pltpu.VMEM((rows, 3 * DH), jnp.float32), keys_t] + rider_space

    def ending(which, q, before, riders):
        return call(
            functools.partial(end_kernel, which=which, index=chips),
            state_of(rows + (short_rows // 2 if riders else 0), 2 * DH),
            (seen, slot, q, end, before, *riders),
            "end",
            end_space,
            len(riders),
        )

    other = across(ending(1, other_queries, other, riders))
    state = ending(0, queries, state, [])
    prompt_out, short_out = call(
        merge_kernel,
        (jax.ShapeDtypeStruct((rows, DH), jnp.bfloat16), jax.ShapeDtypeStruct((short_rows, DH), jnp.bfloat16)),
        (slot, state, other, *riders),
        "merge",
        rider_space,
        len(riders),
    )
    return (prompt_out[None], short_out[None])


def solution(mesh):
    placed = (
        P("inst", None, "sp"),
        P("inst", "sp", None),
        P("inst", "sp", None),
        P(),
        P("inst", None, "sp"),
        P("inst", "sp", None),
        P("inst", "sp", None),
        P(),
        P(),
    )
    return jax.shard_map(
        body,
        mesh=mesh,
        in_specs=placed,
        out_specs=(P("inst", None, "sp"), P("inst", None, "sp")),
        check_vma=False,
    )
```

```python
import functools

import jax
import jax.numpy as jnp
from jax import lax
from jax.experimental import pallas as pl
from jax.experimental.pallas import tpu as pltpu
from jax.sharding import PartitionSpec as P

DH = 128
QH = 32
KVH = 4
CORES = 2
TILE = 128
SHORT_TILE = 256
LOG2E = 1.4426950408889634
GAIN = DH ** (-0.5) * LOG2E
VMEM = 24 * 1024 * 1024
COST = {"load": 10**9, "own": 2 * 10**9, "ring": 4 * 10**9, "end": 10**9, "merge": 10**9}
SMEM_SPEC = pl.BlockSpec(memory_space=pltpu.SMEM)
VMEM_SPEC = pl.BlockSpec(memory_space=pltpu.VMEM)


def with_ones(values):
    return jnp.concatenate([values, jnp.ones_like(values)], axis=1)


def scores_of(q, keys):
    return lax.dot_general(q, keys, (((1,), (1,)), ((), ())), preferred_element_type=jnp.float32)


def weigh(weights, values):
    return jnp.dot(
        weights.astype(jnp.bfloat16), with_ones(values), preferred_element_type=jnp.float32
    )


def add_block(q_ref, keys_t, values, state):
    tiles = [pl.ds(start, TILE) for start in range(0, q_ref.shape[0], TILE)]
    values = with_ones(values)
    scores = [jnp.dot(q_ref[rows, :], keys_t, preferred_element_type=jnp.float32) for rows in tiles]
    olds = [state[rows, 2 * DH : 2 * DH + 1] for rows in tiles]
    parts = []
    for score, old in zip(scores, olds):
        new = jnp.maximum(old, jnp.max(score, axis=1, keepdims=True))
        weights = jnp.exp2((score - new) * GAIN).astype(jnp.bfloat16)
        parts.append((new, jnp.exp2((old - new) * GAIN), weights))
    for rows, (new, factor, weights) in zip(tiles, parts):
        added = jnp.dot(weights, values, preferred_element_type=jnp.float32)
        state[rows, : 2 * DH] = state[rows, : 2 * DH] * factor + added
        state[rows, 2 * DH :] = jnp.broadcast_to(new, (TILE, DH))


def diagonal(q_ref, keys_t, kv_ref, state):
    for start in range(0, q_ref.shape[0], TILE):
        rows = pl.ds(start, TILE)
        seen = start + TILE
        scores = jnp.dot(q_ref[rows, :], keys_t[:, :seen], preferred_element_type=jnp.float32)
        row = start + lax.broadcasted_iota(jnp.int32, scores.shape, 0)
        col = lax.broadcasted_iota(jnp.int32, scores.shape, 1)
        scores = jnp.where(col <= row, scores, -jnp.inf)
        top = jnp.max(scores, axis=1, keepdims=True)
        weights = jnp.exp2((scores - top) * GAIN)
        state[rows, : 2 * DH] = weigh(weights, kv_ref[:seen, DH:])
        state[rows, 2 * DH :] = jnp.broadcast_to(top, (TILE, DH))


def own_kernel(seen_ref, q_ref, other_q_ref, kv_ref, far_ref, state, other, keys_t):
    keys_t[...] = kv_ref[: q_ref.shape[0], :DH].T
    diagonal(q_ref, keys_t, kv_ref, state)
    other[:, : 2 * DH] = jnp.zeros((other.shape[0], 2 * DH), jnp.float32)
    other[:, 2 * DH :] = jnp.full((other.shape[0], DH), -jnp.inf, jnp.float32)

    @pl.when(seen_ref[1, 0] > 0)
    def _():
        add_block(other_q_ref, keys_t[...], kv_ref[: q_ref.shape[0], DH:], other)

    both_sides(seen_ref, seen_ref.shape[1] - 1, q_ref, other_q_ref, far_ref, state, other, keys_t)


def both_sides(seen_ref, index, q_ref, other_q_ref, kv_ref, state, other, keys_t):
    rows = q_ref.shape[0]

    @pl.when((seen_ref[0, index] > 0) | (seen_ref[1, index] > 0))
    def _():
        keys_t[...] = kv_ref[:rows, :DH].T

    @pl.when(seen_ref[0, index] > 0)
    def _():
        add_block(q_ref, keys_t[...], kv_ref[:rows, DH:], state)

    @pl.when(seen_ref[1, index] > 0)
    def _():
        add_block(other_q_ref, keys_t[...], kv_ref[:rows, DH:], other)


def ring_kernel(seen_ref, q_ref, other_q_ref, *refs, indices):
    kv_refs, (before, other_before, state, other, keys_t) = refs[:-5], refs[-5:]
    state[...] = before[...]
    other[...] = other_before[...]
    for index, kv_ref in zip(indices, kv_refs):
        both_sides(seen_ref, index, q_ref, other_q_ref, kv_ref, state, other, keys_t)


def fetch(slot, riders, target, sem):
    for k, ref in enumerate(riders):

        @pl.when(slot == k)
        def _():
            load = pltpu.make_async_copy(ref.at[pl.ds(ref.shape[0] - target.shape[0], target.shape[0]), :], target, sem)
            load.start()
            load.wait()


def end_kernel(seen_ref, slot_ref, q_ref, kv_ref, before, *refs, which, index):
    riders, (packed, state, keys_t, rider, sem) = refs[:-5], refs[-5:]
    rows = q_ref.shape[0]
    state[...] = before[...]

    @pl.when(seen_ref[which, index] > 0)
    def _():
        keys_t[...] = kv_ref[:rows, :DH].T
        add_block(q_ref, keys_t[...], kv_ref[:rows, DH:], state)

    packed[:rows, :DH] = state[:, :DH]
    lane = lax.broadcasted_iota(jnp.int32, (rows, DH), 1)
    packed[:rows, DH:] = jnp.where(lane < DH // 2, state[:, DH : 2 * DH], state[:, 2 * DH :])
    if riders:
        rider[...] = jnp.zeros(rider.shape, rider.dtype)
        fetch(slot_ref[which], riders, rider, sem)
        packed[rows:, :] = rider[...].astype(jnp.float32)


def merge_kernel(slot_ref, mine_ref, other_ref, *refs):
    riders, (out, short_out, rider, sem) = refs[:-4], refs[-4:]
    total = out.shape[0]
    rider[...] = other_ref[total:, :].astype(jnp.bfloat16)
    fetch(slot_ref[0], riders, rider, sem)
    half = rider.shape[0]
    short_out[:half, :] = rider[:, :DH]
    short_out[half:, :] = rider[:, DH:]
    for start in range(0, total, TILE):
        rows = pl.ds(start, TILE)
        mine = mine_ref[rows, 2 * DH - 1 :]
        other = other_ref[rows, 2 * DH - 1 :]
        top = jnp.maximum(mine, other)
        mine = jnp.exp2((mine - top) * GAIN)
        other = jnp.exp2((other - top) * GAIN)
        sums = mine_ref[rows, :DH] * mine + other_ref[rows, :DH] * other
        weight = mine_ref[rows, DH : DH + 1] * mine + other_ref[rows, DH : DH + 1] * other
        out[rows, :] = (sums / weight).astype(jnp.bfloat16)


def load_kernel(ends_ref, q_ref, kv_ref, own_ref, out_ref):
    out_ref[: own_ref.shape[0], :] = own_ref[...]
    half = q_ref.shape[0] // 2
    for start in range(0, q_ref.shape[0], SHORT_TILE):
        rows = pl.ds(start, SHORT_TILE)
        seen = start + SHORT_TILE
        scores = scores_of(q_ref[rows, :], kv_ref[:seen, :DH])
        row = start + lax.broadcasted_iota(jnp.int32, (SHORT_TILE, 1), 0)
        first = jnp.zeros((SHORT_TILE, 1), jnp.int32)
        for k in range(ends_ref.shape[0]):
            first = jnp.where(row >= ends_ref[k], ends_ref[k], first)
        col = lax.broadcasted_iota(jnp.int32, scores.shape, 1)
        scores = jnp.where((col <= row) & (col >= first), scores, -jnp.inf)
        top = jnp.max(scores, axis=1, keepdims=True)
        weights = jnp.exp2((scores - top) * GAIN)
        acc = weigh(weights, kv_ref[:seen, DH:])
        columns = slice(0, DH) if start < half else slice(DH, 2 * DH)
        place = pl.ds(own_ref.shape[0] + start % half, SHORT_TILE)
        out_ref[place, columns] = (acc[:, :DH] / acc[:, DH:]).astype(jnp.bfloat16)


def call(kernel, out_shape, operands, name, scratch=(), left=0):
    specs = [SMEM_SPEC if x.dtype == jnp.int32 else VMEM_SPEC for x in operands]
    return pl.pallas_call(
        kernel,
        out_shape=out_shape,
        in_specs=specs[: len(specs) - left] + [pl.BlockSpec(memory_space=pl.ANY)] * left,
        out_specs=jax.tree.map(lambda _: VMEM_SPEC, out_shape),
        scratch_shapes=scratch,
        compiler_params=pltpu.CompilerParams(vmem_limit_bytes=VMEM),
        cost_estimate=pl.CostEstimate(flops=COST[name], bytes_accessed=1, transcendentals=0),
        name=name,
    )(*operands)


def plan_kernel(me_ref, span_ref, partner_ref, lengths_ref, seen_ref, slot_ref, ends_ref):
    groups = span_ref.shape[0]
    chips = groups // CORES
    me = me_ref[0]
    core = lax.rem(me, CORES)
    for which in range(CORES):
        rows = me if which == 0 else me + 1 - 2 * core
        wanted = partner_ref[rows]
        slot = jnp.int32(chips)
        for k in range(chips + 1):
            chip = lax.rem(me // CORES + (k // 2) * (2 * core - 1) + chips, chips)
            held = chip * CORES + (core if k % 2 == 0 else 1 - core)
            seen_ref[which, k] = (span_ref[held] < span_ref[rows]).astype(jnp.int32)
            if k != 1:
                slot = jnp.where(held == wanted, max(k - 1, 0), slot)
        slot_ref[which] = slot
    total = jnp.int32(0)
    for k in range(lengths_ref.shape[1]):
        total = total + lengths_ref[me, k]
        ends_ref[k] = total


def state_of(rows, width=3 * DH):
    return jax.ShapeDtypeStruct((rows, width), jnp.float32)


def heads_kernel(short_keys, short_values, keys, values, out):
    cut = short_keys.shape[0]
    copies = out.shape[0] // KVH
    for head in range(KVH):
        columns = slice(head * DH, (head + 1) * DH)
        block = jnp.concatenate(
            [
                jnp.concatenate([short_keys[:, columns], short_values[:, columns]], axis=1),
                jnp.concatenate([keys[:, columns], values[:, columns]], axis=1),
            ],
            axis=0,
        )
        for copy in range(copies):
            out[head * copies + copy] = block


def far_heads_kernel(both, out):
    copies = out.shape[0] // KVH
    half = both.shape[1] // 2
    for head in range(KVH):
        keys = both[:, head * DH : (head + 1) * DH]
        values = both[:, half + head * DH : half + (head + 1) * DH]
        block = jnp.concatenate([keys, values], axis=1)
        for copy in range(copies):
            out[head * copies + copy] = block


def swapped(blocks, axis):
    return lax.all_to_all(blocks, axis, split_axis=0, concat_axis=0, tiled=True)


def across(block):
    return lax.ppermute(block, "inst", [(i, i ^ 1) for i in range(lax.axis_size("inst"))])


def opposite(block):
    size = lax.axis_size("inst")
    return lax.ppermute(block, "inst", [(i, (i + size // 2) % size) for i in range(size)])


def ahead(block, crossing=False, chips=1):
    size = lax.axis_size("inst")
    step = lambda i: chips * (CORES if (i + crossing) % CORES == 0 else -CORES)
    return lax.ppermute(block, "inst", [(i, ((i ^ 1 if crossing else i) + step(i)) % size) for i in range(size)])


def body(
    prompt_queries,
    prompt_keys,
    prompt_values,
    span_of,
    short_queries,
    short_keys,
    short_values,
    short_lengths,
    pair_partner,
):
    groups = lax.axis_size("inst")
    chips = groups // CORES
    me = lax.axis_index("inst")
    rows = prompt_queries.shape[1]
    short_rows = short_queries.shape[1]
    queries = prompt_queries[0]

    cut = short_keys.shape[1]
    heads = pl.pallas_call(
        heads_kernel,
        out_shape=jax.ShapeDtypeStruct(
            (lax.axis_size("sp"), cut + prompt_keys.shape[1], 2 * DH), jnp.bfloat16
        ),
        name="heads",
    )(short_keys[0], short_values[0], prompt_keys[0], prompt_values[0])
    got = swapped(heads, "sp")
    short_own = got[:, :cut].reshape(short_rows, 2 * DH)
    own = got[:, cut:].reshape(rows, 2 * DH)
    ints = lambda *shape: jax.ShapeDtypeStruct(shape, jnp.int32)
    seen, slot, ends = pl.pallas_call(
        plan_kernel,
        out_shape=(ints(CORES, chips + 1), ints(CORES), ints(short_lengths.shape[1])),
        in_specs=[SMEM_SPEC] * 4,
        out_specs=(SMEM_SPEC,) * 3,
        name="plan",
    )(me[None], span_of, pair_partner, short_lengths)
    far = opposite(jnp.concatenate([prompt_keys[0], prompt_values[0]], axis=1))
    own, short_own, other_queries, far = lax.optimization_barrier((own, short_own, across(queries), far))
    far = pl.pallas_call(
        far_heads_kernel,
        out_shape=jax.ShapeDtypeStruct((lax.axis_size("sp"), prompt_keys.shape[1], 2 * DH), jnp.bfloat16),
        name="far_heads",
    )(far)
    far = swapped(far, "sp").reshape(rows, 2 * DH)
    load = call(
        load_kernel,
        jax.ShapeDtypeStruct((rows + short_rows // 2, 2 * DH), jnp.bfloat16),
        (ends, short_queries[0], short_own, own),
        "load",
    )
    keys_t = pltpu.VMEM((DH, rows), jnp.bfloat16)
    both = (state_of(rows), state_of(rows))

    def ring_step(step, blocks, states):
        return call(
            functools.partial(ring_kernel, indices=(2 * step, 2 * step + 1)[: len(blocks)]),
            both,
            (seen, queries, other_queries, *blocks, *states),
            "ring",
            [keys_t],
        )

    states = call(own_kernel, both, (seen, queries, other_queries, load, far), "own", [keys_t])
    ring = [(load,), (ahead(load), ahead(load, crossing=True))]
    ring.append(tuple(ahead(block) for block in ring[1]))
    even, states = lax.optimization_barrier((ring[2][0], states))
    last_rider, odd = lax.optimization_barrier((even[rows:], ring[2][1]))
    ring.append((ahead(even), ahead(odd)))
    last_rider = ahead(last_rider, chips=2)
    states = ring_step(1, ring[1], states)
    states = ring_step(2, ring[2], states)
    state, other = ring_step(3, ring[3][:1], states)
    end = ring[3][1]

    riders = [block for pair in ring for block in pair] + [last_rider]
    rider_space = [pltpu.VMEM((short_rows // 2, 2 * DH), jnp.bfloat16), pltpu.SemaphoreType.DMA]
    end_space = [pltpu.VMEM((rows, 3 * DH), jnp.float32), keys_t] + rider_space

    def ending(which, q, before, riders):
        return call(
            functools.partial(end_kernel, which=which, index=chips - 1),
            state_of(rows + (short_rows // 2 if riders else 0), 2 * DH),
            (seen, slot, q, end, before, *riders),
            "end",
            end_space,
            len(riders),
        )

    other = across(ending(1, other_queries, other, riders))
    state = ending(0, queries, state, [])
    prompt_out, short_out = call(
        merge_kernel,
        (jax.ShapeDtypeStruct((rows, DH), jnp.bfloat16), jax.ShapeDtypeStruct((short_rows, DH), jnp.bfloat16)),
        (slot, state, other, *riders),
        "merge",
        rider_space,
        len(riders),
    )
    return (prompt_out[None], short_out[None])


def solution(mesh):
    placed = (
        P("inst", None, "sp"),
        P("inst", "sp", None),
        P("inst", "sp", None),
        P(),
        P("inst", None, "sp"),
        P("inst", "sp", None),
        P("inst", "sp", None),
        P(),
        P(),
    )
    return jax.shard_map(
        body,
        mesh=mesh,
        in_specs=placed,
        out_specs=(P("inst", None, "sp"), P("inst", None, "sp")),
        check_vma=False,
    )
```

```python
import functools

import jax
import jax.numpy as jnp
from jax import lax
from jax.experimental import pallas as pl
from jax.experimental.pallas import tpu as pltpu
from jax.sharding import PartitionSpec as P

DH = 128
QH = 32
KVH = 4
CORES = 2
TILE = 128
SHORT_TILE = 256
LOG2E = 1.4426950408889634
GAIN = DH ** (-0.5) * LOG2E
VMEM = 24 * 1024 * 1024
COST = {"load": 10**9, "own": 2 * 10**9, "ring": 4 * 10**9, "end": 10**9, "merge": 10**9}
SMEM_SPEC = pl.BlockSpec(memory_space=pltpu.SMEM)
VMEM_SPEC = pl.BlockSpec(memory_space=pltpu.VMEM)


def with_ones(values):
    return jnp.concatenate([values, jnp.ones_like(values)], axis=1)


def scores_of(q, keys):
    return lax.dot_general(q, keys, (((1,), (1,)), ((), ())), preferred_element_type=jnp.float32)


def weigh(weights, values):
    return jnp.dot(
        weights.astype(jnp.bfloat16), with_ones(values), preferred_element_type=jnp.float32
    )


def add_block(q_ref, keys_t, values, state):
    tiles = [pl.ds(start, TILE) for start in range(0, q_ref.shape[0], TILE)]
    values = with_ones(values)
    scores = [jnp.dot(q_ref[rows, :], keys_t, preferred_element_type=jnp.float32) for rows in tiles]
    olds = [state[rows, 2 * DH : 2 * DH + 1] for rows in tiles]
    parts = []
    for score, old in zip(scores, olds):
        new = jnp.maximum(old, jnp.max(score, axis=1, keepdims=True))
        weights = jnp.exp2((score - new) * GAIN).astype(jnp.bfloat16)
        parts.append((new, jnp.exp2((old - new) * GAIN), weights))
    for rows, (new, factor, weights) in zip(tiles, parts):
        added = jnp.dot(weights, values, preferred_element_type=jnp.float32)
        state[rows, : 2 * DH] = state[rows, : 2 * DH] * factor + added
        state[rows, 2 * DH :] = jnp.broadcast_to(new, (TILE, DH))


def diagonal(q_ref, keys_t, kv_ref, state):
    for start in range(0, q_ref.shape[0], TILE):
        rows = pl.ds(start, TILE)
        seen = start + TILE
        scores = jnp.dot(q_ref[rows, :], keys_t[:, :seen], preferred_element_type=jnp.float32)
        row = start + lax.broadcasted_iota(jnp.int32, scores.shape, 0)
        col = lax.broadcasted_iota(jnp.int32, scores.shape, 1)
        scores = jnp.where(col <= row, scores, -jnp.inf)
        top = jnp.max(scores, axis=1, keepdims=True)
        weights = jnp.exp2((scores - top) * GAIN)
        state[rows, : 2 * DH] = weigh(weights, kv_ref[:seen, DH:])
        state[rows, 2 * DH :] = jnp.broadcast_to(top, (TILE, DH))


def own_kernel(seen_ref, q_ref, other_q_ref, kv_ref, far_ref, state, other, keys_t):
    keys_t[...] = kv_ref[: q_ref.shape[0], :DH].T
    diagonal(q_ref, keys_t, kv_ref, state)
    other[:, : 2 * DH] = jnp.zeros((other.shape[0], 2 * DH), jnp.float32)
    other[:, 2 * DH :] = jnp.full((other.shape[0], DH), -jnp.inf, jnp.float32)

    @pl.when(seen_ref[1, 0] > 0)
    def _():
        add_block(other_q_ref, keys_t[...], kv_ref[: q_ref.shape[0], DH:], other)

    both_sides(seen_ref, seen_ref.shape[1] - 1, q_ref, other_q_ref, far_ref, state, other, keys_t)


def both_sides(seen_ref, index, q_ref, other_q_ref, kv_ref, state, other, keys_t):
    rows = q_ref.shape[0]

    @pl.when((seen_ref[0, index] > 0) | (seen_ref[1, index] > 0))
    def _():
        keys_t[...] = kv_ref[:rows, :DH].T

    @pl.when(seen_ref[0, index] > 0)
    def _():
        add_block(q_ref, keys_t[...], kv_ref[:rows, DH:], state)

    @pl.when(seen_ref[1, index] > 0)
    def _():
        add_block(other_q_ref, keys_t[...], kv_ref[:rows, DH:], other)


def ring_kernel(seen_ref, q_ref, other_q_ref, *refs, indices):
    kv_refs, (before, other_before, state, other, keys_t) = refs[:-5], refs[-5:]
    state[...] = before[...]
    other[...] = other_before[...]
    for index, kv_ref in zip(indices, kv_refs):
        both_sides(seen_ref, index, q_ref, other_q_ref, kv_ref, state, other, keys_t)


def fetch(slot, riders, target, sem, act):
    for k, ref in enumerate(riders):

        @pl.when(slot == k)
        def _():
            rows = target.shape[0]
            load = pltpu.make_async_copy(ref.at[pl.ds(ref.shape[0] - rows, rows), :], target, sem)
            getattr(load, act)()


def end_kernel(seen_ref, slot_ref, q_ref, kv_ref, before, *refs, which, index):
    riders, (packed, state, keys_t, rider, sem) = refs[:-5], refs[-5:]
    rows = q_ref.shape[0]
    if riders:
        rider[...] = jnp.zeros(rider.shape, rider.dtype)
        fetch(slot_ref[which], riders, rider, sem, "start")
    state[...] = before[...]

    @pl.when(seen_ref[which, index] > 0)
    def _():
        keys_t[...] = kv_ref[:rows, :DH].T
        add_block(q_ref, keys_t[...], kv_ref[:rows, DH:], state)

    packed[:rows, :DH] = state[:, :DH]
    lane = lax.broadcasted_iota(jnp.int32, (rows, DH), 1)
    packed[:rows, DH:] = jnp.where(lane < DH // 2, state[:, DH : 2 * DH], state[:, 2 * DH :])
    if riders:
        fetch(slot_ref[which], riders, rider, sem, "wait")
        packed[rows:, :] = rider[...].astype(jnp.float32)


def merge_kernel(slot_ref, mine_ref, other_ref, *refs):
    riders, (out, short_out, rider, sem) = refs[:-4], refs[-4:]
    total = out.shape[0]
    rider[...] = other_ref[total:, :].astype(jnp.bfloat16)
    fetch(slot_ref[0], riders, rider, sem, "start")
    for start in range(0, total, TILE):
        rows = pl.ds(start, TILE)
        mine = mine_ref[rows, 2 * DH - 1 :]
        other = other_ref[rows, 2 * DH - 1 :]
        top = jnp.maximum(mine, other)
        mine = jnp.exp2((mine - top) * GAIN)
        other = jnp.exp2((other - top) * GAIN)
        sums = mine_ref[rows, :DH] * mine + other_ref[rows, :DH] * other
        weight = mine_ref[rows, DH : DH + 1] * mine + other_ref[rows, DH : DH + 1] * other
        out[rows, :] = (sums / weight).astype(jnp.bfloat16)
    fetch(slot_ref[0], riders, rider, sem, "wait")
    half = rider.shape[0]
    short_out[:half, :] = rider[:, :DH]
    short_out[half:, :] = rider[:, DH:]


def load_kernel(ends_ref, q_ref, kv_ref, own_ref, out_ref):
    out_ref[: own_ref.shape[0], :] = own_ref[...]
    half = q_ref.shape[0] // 2
    for start in range(0, q_ref.shape[0], SHORT_TILE):
        rows = pl.ds(start, SHORT_TILE)
        seen = start + SHORT_TILE
        scores = scores_of(q_ref[rows, :], kv_ref[:seen, :DH])
        row = start + lax.broadcasted_iota(jnp.int32, (SHORT_TILE, 1), 0)
        first = jnp.zeros((SHORT_TILE, 1), jnp.int32)
        for k in range(ends_ref.shape[0]):
            first = jnp.where(row >= ends_ref[k], ends_ref[k], first)
        col = lax.broadcasted_iota(jnp.int32, scores.shape, 1)
        scores = jnp.where((col <= row) & (col >= first), scores, -jnp.inf)
        top = jnp.max(scores, axis=1, keepdims=True)
        weights = jnp.exp2((scores - top) * GAIN)
        acc = weigh(weights, kv_ref[:seen, DH:])
        columns = slice(0, DH) if start < half else slice(DH, 2 * DH)
        place = pl.ds(own_ref.shape[0] + start % half, SHORT_TILE)
        out_ref[place, columns] = (acc[:, :DH] / acc[:, DH:]).astype(jnp.bfloat16)


def call(kernel, out_shape, operands, name, scratch=(), left=0):
    specs = [SMEM_SPEC if x.dtype == jnp.int32 else VMEM_SPEC for x in operands]
    return pl.pallas_call(
        kernel,
        out_shape=out_shape,
        in_specs=specs[: len(specs) - left] + [pl.BlockSpec(memory_space=pl.ANY)] * left,
        out_specs=jax.tree.map(lambda _: VMEM_SPEC, out_shape),
        scratch_shapes=scratch,
        compiler_params=pltpu.CompilerParams(vmem_limit_bytes=VMEM),
        cost_estimate=pl.CostEstimate(flops=COST[name], bytes_accessed=1, transcendentals=0),
        name=name,
    )(*operands)


def plan_kernel(me_ref, span_ref, partner_ref, lengths_ref, seen_ref, slot_ref, ends_ref):
    groups = span_ref.shape[0]
    chips = groups // CORES
    me = me_ref[0]
    core = lax.rem(me, CORES)
    for which in range(CORES):
        rows = me if which == 0 else me + 1 - 2 * core
        wanted = partner_ref[rows]
        slot = jnp.int32(chips)
        for k in range(chips + 1):
            chip = lax.rem(me // CORES + (k // 2) * (2 * core - 1) + chips, chips)
            held = chip * CORES + (core if k % 2 == 0 else 1 - core)
            seen_ref[which, k] = (span_ref[held] < span_ref[rows]).astype(jnp.int32)
            if k != 1:
                slot = jnp.where(held == wanted, max(k - 1, 0), slot)
        slot_ref[which] = slot
    total = jnp.int32(0)
    for k in range(lengths_ref.shape[1]):
        total = total + lengths_ref[me, k]
        ends_ref[k] = total


def state_of(rows, width=3 * DH):
    return jax.ShapeDtypeStruct((rows, width), jnp.float32)


def heads_kernel(short_keys, short_values, keys, values, out):
    cut = short_keys.shape[0]
    copies = out.shape[0] // KVH
    for head in range(KVH):
        columns = slice(head * DH, (head + 1) * DH)
        block = jnp.concatenate(
            [
                jnp.concatenate([short_keys[:, columns], short_values[:, columns]], axis=1),
                jnp.concatenate([keys[:, columns], values[:, columns]], axis=1),
            ],
            axis=0,
        )
        for copy in range(copies):
            out[head * copies + copy] = block


def far_heads_kernel(both, out):
    copies = out.shape[0] // KVH
    half = both.shape[1] // 2
    for head in range(KVH):
        keys = both[:, head * DH : (head + 1) * DH]
        values = both[:, half + head * DH : half + (head + 1) * DH]
        block = jnp.concatenate([keys, values], axis=1)
        for copy in range(copies):
            out[head * copies + copy] = block


def swapped(blocks, axis):
    return lax.all_to_all(blocks, axis, split_axis=0, concat_axis=0, tiled=True)


def across(block):
    return lax.ppermute(block, "inst", [(i, i ^ 1) for i in range(lax.axis_size("inst"))])


def opposite(block):
    size = lax.axis_size("inst")
    return lax.ppermute(block, "inst", [(i, (i + size // 2) % size) for i in range(size)])


def ahead(block, crossing=False, chips=1):
    size = lax.axis_size("inst")
    step = lambda i: chips * (CORES if (i + crossing) % CORES == 0 else -CORES)
    return lax.ppermute(block, "inst", [(i, ((i ^ 1 if crossing else i) + step(i)) % size) for i in range(size)])


def body(
    prompt_queries,
    prompt_keys,
    prompt_values,
    span_of,
    short_queries,
    short_keys,
    short_values,
    short_lengths,
    pair_partner,
):
    groups = lax.axis_size("inst")
    chips = groups // CORES
    me = lax.axis_index("inst")
    rows = prompt_queries.shape[1]
    short_rows = short_queries.shape[1]
    queries = prompt_queries[0]

    cut = short_keys.shape[1]
    heads = pl.pallas_call(
        heads_kernel,
        out_shape=jax.ShapeDtypeStruct(
            (lax.axis_size("sp"), cut + prompt_keys.shape[1], 2 * DH), jnp.bfloat16
        ),
        name="heads",
    )(short_keys[0], short_values[0], prompt_keys[0], prompt_values[0])
    got = swapped(heads, "sp")
    short_own = got[:, :cut].reshape(short_rows, 2 * DH)
    own = got[:, cut:].reshape(rows, 2 * DH)
    ints = lambda *shape: jax.ShapeDtypeStruct(shape, jnp.int32)
    seen, slot, ends = pl.pallas_call(
        plan_kernel,
        out_shape=(ints(CORES, chips + 1), ints(CORES), ints(short_lengths.shape[1])),
        in_specs=[SMEM_SPEC] * 4,
        out_specs=(SMEM_SPEC,) * 3,
        name="plan",
    )(me[None], span_of, pair_partner, short_lengths)
    far = opposite(jnp.concatenate([prompt_keys[0], prompt_values[0]], axis=1))
    own, short_own, other_queries, far = lax.optimization_barrier((own, short_own, across(queries), far))
    far = pl.pallas_call(
        far_heads_kernel,
        out_shape=jax.ShapeDtypeStruct((lax.axis_size("sp"), prompt_keys.shape[1], 2 * DH), jnp.bfloat16),
        name="far_heads",
    )(far)
    far = swapped(far, "sp").reshape(rows, 2 * DH)
    load = call(
        load_kernel,
        jax.ShapeDtypeStruct((rows + short_rows // 2, 2 * DH), jnp.bfloat16),
        (ends, short_queries[0], short_own, own),
        "load",
    )
    keys_t = pltpu.VMEM((DH, rows), jnp.bfloat16)
    both = (state_of(rows), state_of(rows))

    def ring_step(step, blocks, states):
        return call(
            functools.partial(ring_kernel, indices=(2 * step, 2 * step + 1)[: len(blocks)]),
            both,
            (seen, queries, other_queries, *blocks, *states),
            "ring",
            [keys_t],
        )

    states = call(own_kernel, both, (seen, queries, other_queries, load, far), "own", [keys_t])
    ring = [(load,), lax.optimization_barrier((ahead(load), ahead(load, crossing=True)))]
    ring.append(tuple(ahead(block) for block in ring[1]))
    even, states = lax.optimization_barrier((ring[2][0], states))
    states = ring_step(1, ring[1], states)
    last_rider, odd, states = lax.optimization_barrier((even[rows:], ring[2][1], states))
    ring.append((ahead(even), ahead(odd)))
    last_rider = ahead(last_rider, chips=2)
    states = ring_step(2, ring[2], states)
    state, other = ring_step(3, ring[3][:1], states)
    end = ring[3][1]

    riders = [block for pair in ring for block in pair] + [last_rider]
    rider_space = [pltpu.VMEM((short_rows // 2, 2 * DH), jnp.bfloat16), pltpu.SemaphoreType.DMA]
    end_space = [pltpu.VMEM((rows, 3 * DH), jnp.float32), keys_t] + rider_space

    def ending(which, q, before, riders):
        return call(
            functools.partial(end_kernel, which=which, index=chips - 1),
            state_of(rows + (short_rows // 2 if riders else 0), 2 * DH),
            (seen, slot, q, end, before, *riders),
            "end",
            end_space,
            len(riders),
        )

    other = across(ending(1, other_queries, other, riders))
    state = ending(0, queries, state, [])
    prompt_out, short_out = call(
        merge_kernel,
        (jax.ShapeDtypeStruct((rows, DH), jnp.bfloat16), jax.ShapeDtypeStruct((short_rows, DH), jnp.bfloat16)),
        (slot, state, other, *riders),
        "merge",
        rider_space,
        len(riders),
    )
    return (prompt_out[None], short_out[None])


def solution(mesh):
    placed = (
        P("inst", None, "sp"),
        P("inst", "sp", None),
        P("inst", "sp", None),
        P(),
        P("inst", None, "sp"),
        P("inst", "sp", None),
        P("inst", "sp", None),
        P(),
        P(),
    )
    return jax.shard_map(
        body,
        mesh=mesh,
        in_specs=placed,
        out_specs=(P("inst", None, "sp"), P("inst", None, "sp")),
        check_vma=False,
    )
```

```python
import functools

import jax
import jax.numpy as jnp
from jax import lax
from jax.experimental import pallas as pl
from jax.experimental.pallas import tpu as pltpu
from jax.sharding import PartitionSpec as P

DH = 128
QH = 32
KVH = 4
CORES = 2
TILE = 128
SHORT_TILE = 256
LOG2E = 1.4426950408889634
GAIN = DH ** (-0.5) * LOG2E
VMEM = 24 * 1024 * 1024
COST = {"load": 10**9, "own": 2 * 10**9, "ring": 4 * 10**9, "end": 10**9, "merge": 10**9}
SMEM_SPEC = pl.BlockSpec(memory_space=pltpu.SMEM)
VMEM_SPEC = pl.BlockSpec(memory_space=pltpu.VMEM)


def with_ones(values):
    return jnp.concatenate([values, jnp.ones_like(values)], axis=1)


def scores_of(q, keys):
    return lax.dot_general(q, keys, (((1,), (1,)), ((), ())), preferred_element_type=jnp.float32)


def weigh(weights, values):
    return jnp.dot(
        weights.astype(jnp.bfloat16), with_ones(values), preferred_element_type=jnp.float32
    )


def add_block(q_ref, keys_t, values, state):
    tiles = [pl.ds(start, TILE) for start in range(0, q_ref.shape[0], TILE)]
    values = with_ones(values)
    scores = [jnp.dot(q_ref[rows, :], keys_t, preferred_element_type=jnp.float32) for rows in tiles]
    olds = [state[rows, 2 * DH : 2 * DH + 1] for rows in tiles]
    parts = []
    for score, old in zip(scores, olds):
        new = jnp.maximum(old, jnp.max(score, axis=1, keepdims=True))
        weights = jnp.exp2((score - new) * GAIN).astype(jnp.bfloat16)
        parts.append((new, jnp.exp2((old - new) * GAIN), weights))
    for rows, (new, factor, weights) in zip(tiles, parts):
        added = jnp.dot(weights, values, preferred_element_type=jnp.float32)
        state[rows, : 2 * DH] = state[rows, : 2 * DH] * factor + added
        state[rows, 2 * DH :] = jnp.broadcast_to(new, (TILE, DH))


def diagonal(q_ref, keys_t, kv_ref, state):
    for start in range(0, q_ref.shape[0], TILE):
        rows = pl.ds(start, TILE)
        seen = start + TILE
        scores = jnp.dot(q_ref[rows, :], keys_t[:, :seen], preferred_element_type=jnp.float32)
        row = start + lax.broadcasted_iota(jnp.int32, scores.shape, 0)
        col = lax.broadcasted_iota(jnp.int32, scores.shape, 1)
        scores = jnp.where(col <= row, scores, -jnp.inf)
        top = jnp.max(scores, axis=1, keepdims=True)
        weights = jnp.exp2((scores - top) * GAIN)
        state[rows, : 2 * DH] = weigh(weights, kv_ref[:seen, DH:])
        state[rows, 2 * DH :] = jnp.broadcast_to(top, (TILE, DH))


def own_kernel(seen_ref, q_ref, other_q_ref, kv_ref, far_ref, state, other, keys_t):
    keys_t[...] = kv_ref[: q_ref.shape[0], :DH].T
    diagonal(q_ref, keys_t, kv_ref, state)
    other[:, : 2 * DH] = jnp.zeros((other.shape[0], 2 * DH), jnp.float32)
    other[:, 2 * DH :] = jnp.full((other.shape[0], DH), -jnp.inf, jnp.float32)

    @pl.when(seen_ref[1, 0] > 0)
    def _():
        add_block(other_q_ref, keys_t[...], kv_ref[: q_ref.shape[0], DH:], other)

    both_sides(seen_ref, seen_ref.shape[1] - 1, q_ref, other_q_ref, far_ref, state, other, keys_t)


def both_sides(seen_ref, index, q_ref, other_q_ref, kv_ref, state, other, keys_t):
    rows = q_ref.shape[0]

    @pl.when((seen_ref[0, index] > 0) | (seen_ref[1, index] > 0))
    def _():
        keys_t[...] = kv_ref[:rows, :DH].T

    @pl.when(seen_ref[0, index] > 0)
    def _():
        add_block(q_ref, keys_t[...], kv_ref[:rows, DH:], state)

    @pl.when(seen_ref[1, index] > 0)
    def _():
        add_block(other_q_ref, keys_t[...], kv_ref[:rows, DH:], other)


def ring_kernel(seen_ref, q_ref, other_q_ref, *refs, indices):
    kv_refs, (before, other_before, state, other, keys_t) = refs[:-5], refs[-5:]
    state[...] = before[...]
    other[...] = other_before[...]
    for index, kv_ref in zip(indices, kv_refs):
        both_sides(seen_ref, index, q_ref, other_q_ref, kv_ref, state, other, keys_t)


def fetch(slot, riders, target, sem, act):
    for k, ref in enumerate(riders):

        @pl.when(slot == k)
        def _():
            rows = target.shape[0]
            load = pltpu.make_async_copy(ref.at[pl.ds(ref.shape[0] - rows, rows), :], target, sem)
            getattr(load, act)()


def side_kernel(seen_ref, q_ref, kv_ref, before, state, keys_t, *, which, index):
    rows = q_ref.shape[0]
    state[...] = before[...]

    @pl.when(seen_ref[which, index] > 0)
    def _():
        keys_t[...] = kv_ref[:rows, :DH].T
        add_block(q_ref, keys_t[...], kv_ref[:rows, DH:], state)


def end_kernel(seen_ref, slot_ref, q_ref, *refs, which, indices):
    count = len(indices)
    kv_refs, before, refs = refs[:count], refs[count], refs[count + 1 :]
    riders, (packed, state, keys_t, rider, sem) = refs[:-5], refs[-5:]
    rows = q_ref.shape[0]
    if riders:
        rider[...] = jnp.zeros(rider.shape, rider.dtype)
        fetch(slot_ref[which], riders, rider, sem, "start")
    state[...] = before[...]

    for index, kv_ref in zip(indices, kv_refs):

        @pl.when(seen_ref[which, index] > 0)
        def _():
            keys_t[...] = kv_ref[:rows, :DH].T
            add_block(q_ref, keys_t[...], kv_ref[:rows, DH:], state)

    packed[:rows, :DH] = state[:, :DH]
    lane = lax.broadcasted_iota(jnp.int32, (rows, DH), 1)
    packed[:rows, DH:] = jnp.where(lane < DH // 2, state[:, DH : 2 * DH], state[:, 2 * DH :])
    if riders:
        fetch(slot_ref[which], riders, rider, sem, "wait")
        packed[rows:, :] = rider[...].astype(jnp.float32)


def merge_kernel(slot_ref, mine_ref, other_ref, *refs):
    riders, (out, short_out, rider, sem) = refs[:-4], refs[-4:]
    total = out.shape[0]
    rider[...] = other_ref[total:, :].astype(jnp.bfloat16)
    fetch(slot_ref[0], riders, rider, sem, "start")
    for start in range(0, total, TILE):
        rows = pl.ds(start, TILE)
        mine = mine_ref[rows, 2 * DH - 1 :]
        other = other_ref[rows, 2 * DH - 1 :]
        top = jnp.maximum(mine, other)
        mine = jnp.exp2((mine - top) * GAIN)
        other = jnp.exp2((other - top) * GAIN)
        sums = mine_ref[rows, :DH] * mine + other_ref[rows, :DH] * other
        weight = mine_ref[rows, DH : DH + 1] * mine + other_ref[rows, DH : DH + 1] * other
        out[rows, :] = (sums / weight).astype(jnp.bfloat16)
    fetch(slot_ref[0], riders, rider, sem, "wait")
    half = rider.shape[0]
    short_out[:half, :] = rider[:, :DH]
    short_out[half:, :] = rider[:, DH:]


def load_kernel(ends_ref, q_ref, kv_ref, own_ref, out_ref):
    out_ref[: own_ref.shape[0], :] = own_ref[...]
    half = q_ref.shape[0] // 2
    for start in range(0, q_ref.shape[0], SHORT_TILE):
        rows = pl.ds(start, SHORT_TILE)
        seen = start + SHORT_TILE
        scores = scores_of(q_ref[rows, :], kv_ref[:seen, :DH])
        row = start + lax.broadcasted_iota(jnp.int32, (SHORT_TILE, 1), 0)
        first = jnp.zeros((SHORT_TILE, 1), jnp.int32)
        for k in range(ends_ref.shape[0]):
            first = jnp.where(row >= ends_ref[k], ends_ref[k], first)
        col = lax.broadcasted_iota(jnp.int32, scores.shape, 1)
        scores = jnp.where((col <= row) & (col >= first), scores, -jnp.inf)
        top = jnp.max(scores, axis=1, keepdims=True)
        weights = jnp.exp2((scores - top) * GAIN)
        acc = weigh(weights, kv_ref[:seen, DH:])
        columns = slice(0, DH) if start < half else slice(DH, 2 * DH)
        place = pl.ds(own_ref.shape[0] + start % half, SHORT_TILE)
        out_ref[place, columns] = (acc[:, :DH] / acc[:, DH:]).astype(jnp.bfloat16)


def call(kernel, out_shape, operands, name, scratch=(), left=0):
    specs = [SMEM_SPEC if x.dtype == jnp.int32 else VMEM_SPEC for x in operands]
    return pl.pallas_call(
        kernel,
        out_shape=out_shape,
        in_specs=specs[: len(specs) - left] + [pl.BlockSpec(memory_space=pl.ANY)] * left,
        out_specs=jax.tree.map(lambda _: VMEM_SPEC, out_shape),
        scratch_shapes=scratch,
        compiler_params=pltpu.CompilerParams(vmem_limit_bytes=VMEM),
        cost_estimate=pl.CostEstimate(flops=COST[name], bytes_accessed=1, transcendentals=0),
        name=name,
    )(*operands)


def plan_kernel(me_ref, span_ref, partner_ref, lengths_ref, seen_ref, slot_ref, ends_ref):
    groups = span_ref.shape[0]
    chips = groups // CORES
    me = me_ref[0]
    core = lax.rem(me, CORES)
    for which in range(CORES):
        rows = me if which == 0 else me + 1 - 2 * core
        wanted = partner_ref[rows]
        slot = jnp.int32(chips)
        for k in range(chips + 1):
            chip = lax.rem(me // CORES + (k // 2) * (2 * core - 1) + chips, chips)
            held = chip * CORES + (core if k % 2 == 0 else 1 - core)
            seen_ref[which, k] = (span_ref[held] < span_ref[rows]).astype(jnp.int32)
            if k != 1:
                slot = jnp.where(held == wanted, max(k - 1, 0), slot)
        slot_ref[which] = slot
    total = jnp.int32(0)
    for k in range(lengths_ref.shape[1]):
        total = total + lengths_ref[me, k]
        ends_ref[k] = total


def state_of(rows, width=3 * DH):
    return jax.ShapeDtypeStruct((rows, width), jnp.float32)


def heads_kernel(short_keys, short_values, keys, values, out):
    cut = short_keys.shape[0]
    copies = out.shape[0] // KVH
    for head in range(KVH):
        columns = slice(head * DH, (head + 1) * DH)
        block = jnp.concatenate(
            [
                jnp.concatenate([short_keys[:, columns], short_values[:, columns]], axis=1),
                jnp.concatenate([keys[:, columns], values[:, columns]], axis=1),
            ],
            axis=0,
        )
        for copy in range(copies):
            out[head * copies + copy] = block


def far_heads_kernel(both, out):
    copies = out.shape[0] // KVH
    half = both.shape[1] // 2
    for head in range(KVH):
        keys = both[:, head * DH : (head + 1) * DH]
        values = both[:, half + head * DH : half + (head + 1) * DH]
        block = jnp.concatenate([keys, values], axis=1)
        for copy in range(copies):
            out[head * copies + copy] = block


def swapped(blocks, axis):
    return lax.all_to_all(blocks, axis, split_axis=0, concat_axis=0, tiled=True)


def across(block):
    return lax.ppermute(block, "inst", [(i, i ^ 1) for i in range(lax.axis_size("inst"))])


def opposite(block):
    size = lax.axis_size("inst")
    return lax.ppermute(block, "inst", [(i, (i + size // 2) % size) for i in range(size)])


def ahead(block, crossing=False, chips=1):
    size = lax.axis_size("inst")
    step = lambda i: chips * (CORES if (i + crossing) % CORES == 0 else -CORES)
    return lax.ppermute(block, "inst", [(i, ((i ^ 1 if crossing else i) + step(i)) % size) for i in range(size)])


def body(
    prompt_queries,
    prompt_keys,
    prompt_values,
    span_of,
    short_queries,
    short_keys,
    short_values,
    short_lengths,
    pair_partner,
):
    groups = lax.axis_size("inst")
    chips = groups // CORES
    me = lax.axis_index("inst")
    rows = prompt_queries.shape[1]
    short_rows = short_queries.shape[1]
    queries = prompt_queries[0]

    cut = short_keys.shape[1]
    heads = pl.pallas_call(
        heads_kernel,
        out_shape=jax.ShapeDtypeStruct(
            (lax.axis_size("sp"), cut + prompt_keys.shape[1], 2 * DH), jnp.bfloat16
        ),
        name="heads",
    )(short_keys[0], short_values[0], prompt_keys[0], prompt_values[0])
    got = swapped(heads, "sp")
    short_own = got[:, :cut].reshape(short_rows, 2 * DH)
    own = got[:, cut:].reshape(rows, 2 * DH)
    ints = lambda *shape: jax.ShapeDtypeStruct(shape, jnp.int32)
    seen, slot, ends = pl.pallas_call(
        plan_kernel,
        out_shape=(ints(CORES, chips + 1), ints(CORES), ints(short_lengths.shape[1])),
        in_specs=[SMEM_SPEC] * 4,
        out_specs=(SMEM_SPEC,) * 3,
        name="plan",
    )(me[None], span_of, pair_partner, short_lengths)
    far = opposite(jnp.concatenate([prompt_keys[0], prompt_values[0]], axis=1))
    own, short_own, other_queries, far = lax.optimization_barrier((own, short_own, across(queries), far))
    far = pl.pallas_call(
        far_heads_kernel,
        out_shape=jax.ShapeDtypeStruct((lax.axis_size("sp"), prompt_keys.shape[1], 2 * DH), jnp.bfloat16),
        name="far_heads",
    )(far)
    far = swapped(far, "sp").reshape(rows, 2 * DH)
    load = call(
        load_kernel,
        jax.ShapeDtypeStruct((rows + short_rows // 2, 2 * DH), jnp.bfloat16),
        (ends, short_queries[0], short_own, own),
        "load",
    )
    keys_t = pltpu.VMEM((DH, rows), jnp.bfloat16)
    both = (state_of(rows), state_of(rows))

    def ring_step(step, blocks, states):
        return call(
            functools.partial(ring_kernel, indices=(2 * step, 2 * step + 1)[: len(blocks)]),
            both,
            (seen, queries, other_queries, *blocks, *states),
            "ring",
            [keys_t],
        )

    states = call(own_kernel, both, (seen, queries, other_queries, load, far), "own", [keys_t])
    ring = [(load,), (ahead(load), ahead(load, crossing=True))]
    ring.append(tuple(ahead(block) for block in ring[1]))
    even, states = lax.optimization_barrier((ring[2][0], states))
    last_rider, odd = lax.optimization_barrier((even[rows:], ring[2][1]))
    ring.append((ahead(even), ahead(odd)))
    last_rider = ahead(last_rider, chips=2)
    states = ring_step(1, ring[1], states)
    states = ring_step(2, ring[2], states)
    state, other = states
    other = call(
        functools.partial(side_kernel, which=1, index=chips - 2),
        state_of(rows),
        (seen, other_queries, ring[3][0], other),
        "end",
        [keys_t],
    )
    end = ring[3][1]

    riders = [block for pair in ring for block in pair] + [last_rider]
    rider_space = [pltpu.VMEM((short_rows // 2, 2 * DH), jnp.bfloat16), pltpu.SemaphoreType.DMA]
    end_space = [pltpu.VMEM((rows, 3 * DH), jnp.float32), keys_t] + rider_space

    def ending(which, q, blocks, indices, before, riders):
        return call(
            functools.partial(end_kernel, which=which, indices=indices),
            state_of(rows + (short_rows // 2 if riders else 0), 2 * DH),
            (seen, slot, q, *blocks, before, *riders),
            "end",
            end_space,
            len(riders),
        )

    other = across(ending(1, other_queries, (end,), (chips - 1,), other, riders))
    state = ending(0, queries, (ring[3][0], end), (chips - 2, chips - 1), state, [])
    prompt_out, short_out = call(
        merge_kernel,
        (jax.ShapeDtypeStruct((rows, DH), jnp.bfloat16), jax.ShapeDtypeStruct((short_rows, DH), jnp.bfloat16)),
        (slot, state, other, *riders),
        "merge",
        rider_space,
        len(riders),
    )
    return (prompt_out[None], short_out[None])


def solution(mesh):
    placed = (
        P("inst", None, "sp"),
        P("inst", "sp", None),
        P("inst", "sp", None),
        P(),
        P("inst", None, "sp"),
        P("inst", "sp", None),
        P("inst", "sp", None),
        P(),
        P(),
    )
    return jax.shard_map(
        body,
        mesh=mesh,
        in_specs=placed,
        out_specs=(P("inst", None, "sp"), P("inst", None, "sp")),
        check_vma=False,
    )
```
